1024 devices in a mesh: row: 16 (over y_hi, x), col: 16 (over z, core), rep: 4 (over y_lo).
Axes of the slice: x: 8, y: 8 (y_hi: 2, y_lo: 4; y = y_hi * 4 + y_lo), z: 8, core: 2. Of those that a mesh axis runs over, the one named last changes fastest.
Arguments:
- a_blocks: float32 [16, 16, 4, 16, 128, 128], P('row', 'col', 'rep'), may hold values from -6 to 6
- a_where: int32 [16, 16, 4, 16], P('row', 'col', 'rep'), may hold values from 0 to 255, as said below
- b_blocks: float32 [16, 16, 4, 32, 128, 128], P('row', 'col', 'rep'), may hold values from -0.09375 to 0.09375
- b_where: int32 [16, 16, 4, 32], P('row', 'col', 'rep'), may hold values from 0 to 255, as said below
- c_where: int32 [16, 16, 8], P('row', 'col'), may hold values from 0 to 15, as said below
Outputs:
- c_blocks: float32 [16, 16, 8, 128, 128], P('row', 'col', 'rep')
The draws below stay inside these ranges and needn't reach their ends.
Inputs may be any that keep to these rules, and one draw needn't show every extreme that they name: `a_where`: within one device's list the positions are distinct. Panels (left and right) with the same replica and the same (p + q) mod 16 draw their inner block indices from one common set of 8; each left block row holds 4 blocks of that set, and a right panel holds all 4 blocks of each of its 8 inner block rows. List order is arbitrary. `b_where`: within one device's list the positions are distinct; see a_where for the inner index sets. `c_where`: within one panel's list the positions are distinct.
All inputs are finite; a program needn't handle non-finite values.
Results may differ from the reference program's by a relative error of at most 0.0003.
Values sent between devices are 32-bit elements; how exact they have to be, the bound alone decides.
A program may use at most 32 MiB of HBM per device.

```python
import jax
import jax.numpy as jnp
from jax import lax

BLOCK = 128
RB = 4
KB = 64
CB = 4
KSET = 8
PER_ROW = 4
NA = 16
NB = 32
NC = 8
GRID_ROWS = 16
GRID_COLS = 16
REPLICAS = 4
N_REP = 4


def inner_sets(key):
    keys = jax.random.split(key, GRID_ROWS * REPLICAS)
    sets = jax.vmap(lambda one: jax.random.permutation(one, KB)[:KSET])(keys)
    return sets.reshape(GRID_ROWS, REPLICAS, KSET).astype(jnp.int32)


def device_sets(sets):
    prow = jnp.arange(GRID_ROWS, dtype=jnp.int32)[:, None, None]
    pcol = jnp.arange(GRID_COLS, dtype=jnp.int32)[None, :, None]
    preps = jnp.arange(REPLICAS, dtype=jnp.int32)[None, None, :]
    diagonal = (prow + pcol) % GRID_ROWS
    diagonal = jnp.broadcast_to(diagonal, (GRID_ROWS, GRID_COLS, REPLICAS))
    preps = jnp.broadcast_to(preps, (GRID_ROWS, GRID_COLS, REPLICAS))
    return sets[diagonal, preps]


def shuffle_lists(key, lists, count):
    flat = lists.reshape(-1, count)
    keys = jax.random.split(key, flat.shape[0])
    orders = jax.vmap(lambda one: jax.random.permutation(one, count))(keys)
    return jnp.take_along_axis(flat, orders, axis=-1).reshape(lists.shape).astype(jnp.int32)


def draw_a_where(key, part):
    sets = inner_sets(key)
    key = jax.random.fold_in(key, 11)
    chosen = device_sets(sets)
    keys = jax.random.split(key, GRID_ROWS * GRID_COLS * REPLICAS * RB)
    picks = jax.vmap(lambda one: jax.random.permutation(one, KSET)[:PER_ROW])(keys)
    picks = picks.reshape(GRID_ROWS, GRID_COLS, REPLICAS, RB, PER_ROW).astype(jnp.int32)
    wide = jnp.broadcast_to(chosen[:, :, :, None, :], (GRID_ROWS, GRID_COLS, REPLICAS, RB, KSET))
    inner = jnp.take_along_axis(wide, picks, axis=-1)
    spots = jnp.arange(RB, dtype=jnp.int32)[:, None] * KB + inner
    spots = spots.reshape(GRID_ROWS, GRID_COLS, REPLICAS, NA)
    return shuffle_lists(jax.random.fold_in(key, 5), spots, NA)


def draw_b_where(key, part):
    sets = inner_sets(key)
    key = jax.random.fold_in(key, 23)
    chosen = device_sets(sets)
    spots = chosen[..., :, None] * CB + jnp.arange(CB, dtype=jnp.int32)
    spots = spots.reshape(GRID_ROWS, GRID_COLS, REPLICAS, NB)
    return shuffle_lists(key, spots, NB)


def draw_c_where(key, part):
    key = jax.random.fold_in(key, 37)
    keys = jax.random.split(key, GRID_ROWS * GRID_COLS)
    picked = jax.vmap(lambda one: jax.random.permutation(one, RB * CB)[:NC])(keys)
    return picked.astype(jnp.int32).reshape(GRID_ROWS, GRID_COLS, NC)


def shard_levels(key, dims, cuts, low, top_value):
    def one(axis_at, shards_of):
        heights = jax.random.uniform(jax.random.fold_in(jax.random.fold_in(key, 6), axis_at), (shards_of,), jnp.float32, low / len(cuts), top_value / len(cuts))
        return jnp.repeat(jnp.exp(heights), dims[axis_at] // shards_of).reshape((-1,) + (1,) * (len(dims) - axis_at - 1))

    gain = one(*cuts[0])
    for cut in cuts[1:]:
        gain = gain * one(*cut)
    return gain


def gaussian(key, extent, width, bound, cuts=(), kind=jnp.bfloat16):
    factor_of = shard_levels(key, extent, cuts, -0.22, 0.18) if cuts else 1.0
    values = jax.random.normal(key, extent, jnp.float32) * width * factor_of
    return jnp.minimum(jnp.maximum(values, -bound), bound).astype(kind)


def setup_inputs(seed: int = 0) -> dict:
    seeds = jax.random.split(jax.random.key(seed), 6)
    a_blocks = gaussian(seeds[0], (GRID_ROWS, GRID_COLS, REPLICAS, NA, BLOCK, BLOCK), 1.0, 6.0, ((0, 16), (1, 16), (2, 4)), jnp.float32)
    a_where = draw_a_where(jax.random.fold_in(seeds[5], 71), 0)
    b_blocks = gaussian(seeds[2], (GRID_ROWS, GRID_COLS, REPLICAS, NB, BLOCK, BLOCK), (2 * PER_ROW * BLOCK * N_REP) ** -0.5, 0.09375, ((0, 16), (1, 16), (2, 4)), jnp.float32)
    b_where = draw_b_where(jax.random.fold_in(seeds[5], 71), 0)
    c_where = draw_c_where(jax.random.fold_in(seeds[5], 71), 0)
    return dict(a_blocks=a_blocks, a_where=a_where, b_blocks=b_blocks, b_where=b_where, c_where=c_where)


def kept_product(a_list, a_spots, b_list, b_spots, c_spots):
    a_inner = a_spots % KB
    a_row = a_spots // KB
    b_inner = b_spots // CB
    b_col = b_spots % CB
    columns = jnp.arange(CB, dtype=jnp.int32)
    pick = ((a_inner[:, None, None] == b_inner[None, None, :]) & (b_col[None, None, :] == columns[None, :, None])).astype(jnp.float32)
    matched = jnp.einsum("ajb,bxy->ajxy", pick, b_list, precision=lax.Precision.HIGHEST)
    pieces = jnp.einsum("axy,ajyz->ajxz", a_list, matched, precision=lax.Precision.HIGHEST)
    keep = (((c_spots // CB)[:, None, None] == a_row[None, :, None]) & ((c_spots % CB)[:, None, None] == columns[None, None, :])).astype(jnp.float32)
    return jnp.einsum("saj,ajxz->sxz", keep, pieces, precision=lax.Precision.HIGHEST)


def reference(a_blocks, a_where, b_blocks, b_where, c_where):
    a_next = jnp.roll(a_blocks, -1, axis=1)
    aw_next = jnp.roll(a_where, -1, axis=1)
    b_next = jnp.roll(b_blocks, -1, axis=0)
    bw_next = jnp.roll(b_where, -1, axis=0)

    def one_row(items):
        a_row, aw_row, an_row, awn_row, b_row, bw_row, bn_row, bwn_row, cw_row = items

        def one_panel(q):
            total = jnp.zeros((NC, BLOCK, BLOCK), jnp.float32)
            for rep_index in range(REPLICAS):
                total = total + kept_product(a_row[q, rep_index], aw_row[q, rep_index], b_row[q, rep_index], bw_row[q, rep_index], cw_row[q])
                total = total + kept_product(an_row[q, rep_index], awn_row[q, rep_index], bn_row[q, rep_index], bwn_row[q, rep_index], cw_row[q])
            return total

        return lax.map(one_panel, jnp.arange(GRID_COLS, dtype=jnp.int32))

    return lax.map(one_row, (a_blocks, a_where, a_next, aw_next, b_blocks, b_where, b_next, bw_next, c_where))
```

```python
import functools

import jax
import jax.numpy as jnp
from jax import lax
from jax.experimental import pallas as pl
from jax.experimental.pallas import tpu as pltpu
from jax.sharding import PartitionSpec as P

KB = 64
CB = 4
RB = 4
KSET = 8
NA = 16
NB = 32
NC = 8
BLOCK = 128
CHUNKS = 4
PER_CHUNK = NA // CHUNKS
MESH = pl.DeviceIdType.MESH


def sort_order(where, count, rank, order):
    def rank_one(n, carry):
        mine = where[0, n]
        below = jnp.int32(0)
        for m in range(count):
            below += (where[0, m] < mine).astype(jnp.int32)
        rank[n] = below
        return carry

    lax.fori_loop(0, count, rank_one, 0)

    def place_one(t, carry):
        found = jnp.int32(0)
        for n in range(count):
            found = jnp.where(rank[n] == t, n, found)
        order[t] = found
        return carry

    lax.fori_loop(0, count, place_one, 0)


def split(x):
    high = x.astype(jnp.bfloat16)
    low = (x - high.astype(jnp.float32)).astype(jnp.bfloat16)
    return high, low


def kernel(
    rows, cols, reps,
    a_where, b_where, c_where, a_hbm, b_hbm, aw_hbm, cw_hbm, out,
    a_own, b_own, a_next, aw_land, cw_land, aw_next, cw_next, right, pieces, first, second, got_first, got_second,
    rank, a_order, b_order, inner,
    local_sem, meta_sem, small_send, small_recv, a_send, a_recv, first_send, first_recv, second_send, second_recv,
):
    p, q, r = lax.axis_index("row"), lax.axis_index("col"), lax.axis_index("rep")
    p_up, p_down = lax.rem(p + 1, rows), lax.rem(p + rows - 1, rows)
    q_up, q_down = lax.rem(q + 1, cols), lax.rem(q + cols - 1, cols)
    share = NC // reps

    load_a = pltpu.make_async_copy(a_hbm, a_own, local_sem.at[0])
    load_b = pltpu.make_async_copy(b_hbm, b_own, local_sem.at[1])
    load_b.start()
    load_a.start()

    barrier = pltpu.get_barrier_semaphore()
    pl.semaphore_signal(barrier, inc=1, device_id=(p_down, q_up, r), device_id_type=MESH)
    pl.semaphore_signal(barrier, inc=1, device_id=(p_down, q, r), device_id_type=MESH)
    for d in range(reps):
        there = lax.rem(r + d, reps)
        pl.semaphore_signal(barrier, inc=1, device_id=(p_up, q, there), device_id_type=MESH)
        if d:
            pl.semaphore_signal(barrier, inc=1, device_id=(p, q, there), device_id_type=MESH)
    pl.semaphore_wait(barrier, 2 * reps + 1)

    away = (p_up, q_down, r)
    small = [
        pltpu.make_async_remote_copy(
            src_ref=aw_hbm, dst_ref=aw_land, send_sem=small_send.at[0], recv_sem=small_recv.at[0],
            device_id=away, device_id_type=MESH,
        ),
        pltpu.make_async_remote_copy(
            src_ref=cw_hbm, dst_ref=cw_land, send_sem=small_send.at[1], recv_sem=small_recv.at[1],
            device_id=(p_up, q, r), device_id_type=MESH,
        ),
    ]
    for copy in small:
        copy.start()
    panels = []
    for c in range(CHUNKS):
        part = pl.ds(c * PER_CHUNK, PER_CHUNK)
        copy = pltpu.make_async_remote_copy(
            src_ref=a_hbm.at[part], dst_ref=a_next.at[part], send_sem=a_send.at[c], recv_sem=a_recv.at[c],
            device_id=away, device_id_type=MESH,
        )
        copy.start()
        panels.append(copy)

    sort_order(b_where, NB, rank, b_order)
    load_b.wait()

    def lay_right(u, carry):
        for j in range(CB):
            high, low = split(b_own[b_order[u * CB + j]])
            at = slice(j * BLOCK, (j + 1) * BLOCK)
            right[u, :BLOCK, at] = high
            right[u, BLOCK:, at] = low
        return carry

    lax.fori_loop(0, KSET, lay_right, 0)

    def places(where):
        def one(n, carry):
            k = lax.rem(where[0, n], KB)
            slot = jnp.int32(0)
            for u in range(1, KSET):
                slot += (b_where[0, b_order[u * CB]] <= k * CB).astype(jnp.int32)
            inner[n] = slot
            return carry

        lax.fori_loop(0, NA, one, 0)
        sort_order(where, NA, rank, a_order)

    def multiply(blocks):
        def one(n, carry):
            high, low = split(blocks[n])
            left = jnp.concatenate(
                [jnp.concatenate([high, high], axis=1), jnp.concatenate([low, low], axis=1)], axis=0
            )
            both = jnp.dot(left, right[inner[n]], preferred_element_type=jnp.float32)
            total = both[:BLOCK] + both[BLOCK:]
            for j in range(CB):
                pieces[n * CB + j] = total[:, j * BLOCK:(j + 1) * BLOCK]
            return carry

        return one

    def keep(spots, into, s):
        spot = spots[0, s]
        i, j = spot // CB, lax.rem(spot, CB)
        total = pieces[a_order[i * RB] * CB + j]
        for t in range(1, RB):
            total += pieces[a_order[i * RB + t] * CB + j]
        into[s] = total

    places(a_where)
    load_a.wait()
    lax.fori_loop(0, NA, multiply(a_own), 0)

    def keep_first(s, carry):
        keep(c_where, first, s)
        return carry

    lax.fori_loop(0, NC, keep_first, 0)
    firsts = []
    for d in range(1, reps):
        there = lax.rem(r + d, reps)
        copy = pltpu.make_async_remote_copy(
            src_ref=first.at[pl.ds(there * share, share)], dst_ref=got_first.at[d - 1],
            send_sem=first_send.at[d - 1], recv_sem=first_recv.at[d - 1],
            device_id=(p, q, there), device_id_type=MESH,
        )
        copy.start()
        firsts.append(copy)

    for copy in small:
        copy.wait_recv()
    to_scalars = [
        pltpu.make_async_copy(aw_land, aw_next, meta_sem.at[0]),
        pltpu.make_async_copy(cw_land, cw_next, meta_sem.at[1]),
    ]
    for copy in to_scalars:
        copy.start()
    for copy in to_scalars:
        copy.wait()
    places(aw_next)
    for c in range(CHUNKS):
        panels[c].wait_recv()
        lax.fori_loop(c * PER_CHUNK, (c + 1) * PER_CHUNK, multiply(a_next), 0)
    seconds = []
    for d in range(reps):
        there = lax.rem(r + d, reps)

        def keep_second(s, carry):
            keep(cw_next, second, there * share + s)
            return carry

        lax.fori_loop(0, share, keep_second, 0)
        copy = pltpu.make_async_remote_copy(
            src_ref=second.at[pl.ds(there * share, share)], dst_ref=got_second.at[d],
            send_sem=second_send.at[d], recv_sem=second_recv.at[d],
            device_id=(p_down, q, there), device_id_type=MESH,
        )
        copy.start()
        seconds.append(copy)

    total = first[pl.ds(r * share, share)]
    for d in range(1, reps):
        firsts[d - 1].wait_recv()
        total += got_first[d - 1]
    for d in range(reps):
        seconds[d].wait_recv()
        total += got_second[d]
    out[...] = total
    for copy in small + panels + firsts + seconds:
        copy.wait_send()


def shards(rows, cols, reps, a_blocks, a_where, b_blocks, b_where, c_where):
    share = NC // reps
    a_spots = a_where.reshape(1, NA)
    b_spots = b_where.reshape(1, NB)
    c_spots = c_where.reshape(1, NC)
    smem, hbm, vmem = (pl.BlockSpec(memory_space=m) for m in (pltpu.SMEM, pl.ANY, pltpu.VMEM))
    dma = pltpu.SemaphoreType.DMA
    f32, i32, bf16 = jnp.float32, jnp.int32, jnp.bfloat16
    result = pl.pallas_call(
        functools.partial(kernel, rows, cols, reps),
        out_shape=jax.ShapeDtypeStruct((share, BLOCK, BLOCK), f32),
        in_specs=[smem, smem, smem, hbm, hbm, hbm, hbm],
        out_specs=vmem,
        scratch_shapes=[
            pltpu.VMEM((NA, BLOCK, BLOCK), f32),
            pltpu.VMEM((NB, BLOCK, BLOCK), f32),
            pltpu.VMEM((NA, BLOCK, BLOCK), f32),
            pltpu.VMEM((1, NA), i32),
            pltpu.VMEM((1, NC), i32),
            pltpu.SMEM((1, NA), i32),
            pltpu.SMEM((1, NC), i32),
            pltpu.VMEM((KSET, 2 * BLOCK, CB * BLOCK), bf16),
            pltpu.VMEM((NA * CB, BLOCK, BLOCK), f32),
            pltpu.VMEM((NC, BLOCK, BLOCK), f32),
            pltpu.VMEM((NC, BLOCK, BLOCK), f32),
            pltpu.VMEM((reps - 1, share, BLOCK, BLOCK), f32),
            pltpu.VMEM((reps, share, BLOCK, BLOCK), f32),
            pltpu.SMEM((NB,), i32),
            pltpu.SMEM((NA,), i32),
            pltpu.SMEM((NB,), i32),
            pltpu.SMEM((NA,), i32),
            dma((2,)), dma((2,)), dma((2,)), dma((2,)), dma((CHUNKS,)), dma((CHUNKS,)),
            dma((reps - 1,)), dma((reps - 1,)), dma((reps,)), dma((reps,)),
        ],
        compiler_params=pltpu.CompilerParams(
            collective_id=0, has_side_effects=True, vmem_limit_bytes=60 * 1024 * 1024
        ),
        cost_estimate=pl.CostEstimate(flops=2 * 2 * NA * 4 * CB * BLOCK**3, bytes_accessed=4 << 20, transcendentals=0),
    )(
        a_spots, b_spots, c_spots,
        a_blocks.reshape(NA, BLOCK, BLOCK), b_blocks.reshape(NB, BLOCK, BLOCK), a_spots, c_spots,
    )
    return result[None, None]


def solution(mesh):
    in_specs = (
        P("row", "col", "rep", None, None, None),
        P("row", "col", "rep", None),
        P("row", "col", "rep", None, None, None),
        P("row", "col", "rep", None),
        P("row", "col", None),
    )
    out_specs = P("row", "col", "rep", None, None)
    body = functools.partial(shards, mesh.shape["row"], mesh.shape["col"], mesh.shape["rep"])
    return jax.shard_map(body, mesh=mesh, in_specs=in_specs, out_specs=out_specs, check_vma=False)
```

```python
import functools

import jax
import jax.numpy as jnp
from jax import lax
from jax.experimental import pallas as pl
from jax.experimental.pallas import tpu as pltpu
from jax.sharding import PartitionSpec as P

KB = 64
CB = 4
RB = 4
KSET = 8
NA = 16
NB = 32
NC = 8
BLOCK = 128
CHUNKS = 8
PER_CHUNK = NA // CHUNKS
MESH = pl.DeviceIdType.MESH


def sort_order(where, count, rank, order):
    def rank_one(n, carry):
        mine = where[0, n]
        below = jnp.int32(0)
        for m in range(count):
            below += (where[0, m] < mine).astype(jnp.int32)
        rank[n] = below
        return carry

    lax.fori_loop(0, count, rank_one, 0)

    def place_one(t, carry):
        found = jnp.int32(0)
        for n in range(count):
            found = jnp.where(rank[n] == t, n, found)
        order[t] = found
        return carry

    lax.fori_loop(0, count, place_one, 0)


def split(x):
    high = x.astype(jnp.bfloat16)
    low = (x - high.astype(jnp.float32)).astype(jnp.bfloat16)
    return high, low


def kernel(
    rows, cols, reps,
    a_where, b_where, c_where, a_hbm, b_hbm, aw_hbm, cw_hbm, out,
    a_own, b_own, a_next, via, aw_land, cw_land, aw_next, cw_next, right, pieces, first, second, got_first, got_second,
    rank, a_order, b_order, inner,
    local_sem, meta_sem, small_send, small_recv, a_send, a_recv, via_send, via_recv, first_send, first_recv, second_send, second_recv,
):
    p, q, r = lax.axis_index("row"), lax.axis_index("col"), lax.axis_index("rep")
    p_up, p_down = lax.rem(p + 1, rows), lax.rem(p + rows - 1, rows)
    q_up, q_down = lax.rem(q + 1, cols), lax.rem(q + cols - 1, cols)
    share = NC // reps

    load_a = pltpu.make_async_copy(a_hbm, a_own, local_sem.at[0])
    load_b = pltpu.make_async_copy(b_hbm, b_own, local_sem.at[1])
    load_b.start()
    load_a.start()

    width = rows // 2
    x, half = lax.rem(p, width), p // width
    last, stop, near = width - 1, width // 2, width // 8
    across = lax.rem(p + width, rows)

    def row_at(at, side):
        return side * width + at

    def remote(src, dst, send_sem, recv_sem, device):
        return pltpu.make_async_remote_copy(
            src_ref=src, dst_ref=dst, send_sem=send_sem, recv_sem=recv_sem, device_id=device, device_id_type=MESH
        )

    barrier = pltpu.get_barrier_semaphore()

    def greet(*device):
        pl.semaphore_signal(barrier, inc=1, device_id=device, device_id_type=MESH)

    greet(p_down, q_up, r)
    greet(p_down, q, r)
    for d in range(reps):
        there = lax.rem(r + d, reps)
        greet(p_up, q, there)
        if d:
            greet(p, q, there)

    @pl.when(x == last)
    def _():
        greet(across, q, r)

    @pl.when(x == stop)
    def _():
        greet(row_at(last, 0), q, r)
        greet(row_at(last, 1), q, r)

    @pl.when(x == near)
    def _():
        greet(row_at(stop, 0), q, r)
        greet(row_at(stop, 1), q, r)

    @pl.when(x == 0)
    def _():
        greet(row_at(last, half), q_up, r)
        greet(row_at(near, half), q_up, r)

    more = jnp.where(x == last, 4, jnp.where(x == stop, 2, jnp.where(x == near, 1, 0)))
    pl.semaphore_wait(barrier, 2 * reps + 1 + more)

    away = (p_up, q_down, r)
    small = [
        remote(aw_hbm, aw_land, small_send.at[0], small_recv.at[0], away),
        remote(cw_hbm, cw_land, small_send.at[1], small_recv.at[1], (p_up, q, r)),
    ]
    for copy in small:
        copy.start()

    def part(c):
        return pl.ds(c * PER_CHUNK, PER_CHUNK)

    panels = [
        remote(a_hbm.at[part(c)], a_next.at[part(c)], a_send.at[c], a_recv.at[c], away) for c in range(CHUNKS)
    ]

    def leg(c, at, device):
        return remote(a_hbm.at[part(c)], via.at[part(at)], a_send.at[c], via_recv.at[at], device)

    def pass_on(at, device):
        return remote(via.at[part(at)], via.at[part(at)], via_send.at[at], via_recv.at[at], device)

    def land(at, c, device):
        return remote(via.at[part(at)], a_next.at[part(c)], via_send.at[at], a_recv.at[c], device)

    @pl.when(x != last)
    def _():
        for copy in panels:
            copy.start()

    @pl.when(x == last)
    def _():
        for c in range(2):
            panels[c].start()
            leg(2 + c, c, (across, q, r)).start()
            leg(4 + c, c, (row_at(stop, 1 - half), q, r)).start()
            leg(6 + c, 2 + c, (row_at(stop, half), q, r)).start()

    def at_last():
        return [(c, land(c, 2 + c, (row_at(0, half), q_down, r))) for c in range(2)]

    def at_stop():
        sides = (half, 1 - half)
        return [
            (2 * k + c, pass_on(2 * k + c, (row_at(near, sides[k]), q, r))) for c in range(2) for k in range(2)
        ]

    def at_near():
        return [
            (2 * k + c, land(2 * k + c, 4 + 2 * k + c, (row_at(0, half), q_down, r)))
            for c in range(2) for k in range(2)
        ]

    places_on_way = ((last, at_last), (stop, at_stop), (near, at_near))

    def forward():
        for place, copies in places_on_way:
            @pl.when(x == place)
            def _():
                for at, copy in copies():
                    pass_on(at, away).wait_recv()
                    copy.start()

    def forwarded():
        for place, copies in places_on_way:
            @pl.when(x == place)
            def _():
                for _, copy in copies():
                    copy.wait_send()

    sort_order(b_where, NB, rank, b_order)
    load_b.wait()

    def lay_right(u, carry):
        for j in range(CB):
            high, low = split(b_own[b_order[u * CB + j]])
            at = slice(j * BLOCK, (j + 1) * BLOCK)
            right[u, :BLOCK, at] = high
            right[u, BLOCK:, at] = low
        return carry

    lax.fori_loop(0, KSET, lay_right, 0)

    def places(where):
        def one(n, carry):
            k = lax.rem(where[0, n], KB)
            slot = jnp.int32(0)
            for u in range(1, KSET):
                slot += (b_where[0, b_order[u * CB]] <= k * CB).astype(jnp.int32)
            inner[n] = slot
            return carry

        lax.fori_loop(0, NA, one, 0)
        sort_order(where, NA, rank, a_order)

    def multiply(blocks):
        def one(n, carry):
            high, low = split(blocks[n])
            left = jnp.concatenate(
                [jnp.concatenate([high, high], axis=1), jnp.concatenate([low, low], axis=1)], axis=0
            )
            both = jnp.dot(left, right[inner[n]], preferred_element_type=jnp.float32)
            total = both[:BLOCK] + both[BLOCK:]
            for j in range(CB):
                pieces[n * CB + j] = total[:, j * BLOCK:(j + 1) * BLOCK]
            return carry

        return one

    def keep(spots, into, s):
        spot = spots[0, s]
        i, j = spot // CB, lax.rem(spot, CB)
        total = pieces[a_order[i * RB] * CB + j]
        for t in range(1, RB):
            total += pieces[a_order[i * RB + t] * CB + j]
        into[s] = total

    places(a_where)
    load_a.wait()
    lax.fori_loop(0, NA, multiply(a_own), 0)

    def keep_first(s, carry):
        keep(c_where, first, s)
        return carry

    lax.fori_loop(0, NC, keep_first, 0)
    firsts = [
        remote(
            first.at[pl.ds(lax.rem(r + d, reps) * share, share)], got_first.at[d - 1],
            first_send.at[d - 1], first_recv.at[d - 1], (p, q, lax.rem(r + d, reps)),
        )
        for d in range(1, reps)
    ]
    for copy in firsts:
        copy.start()
    forward()

    for copy in small:
        copy.wait_recv()
    to_scalars = [
        pltpu.make_async_copy(aw_land, aw_next, meta_sem.at[0]),
        pltpu.make_async_copy(cw_land, cw_next, meta_sem.at[1]),
    ]
    for copy in to_scalars:
        copy.start()
    for copy in to_scalars:
        copy.wait()
    places(aw_next)
    for c in range(CHUNKS):
        panels[c].wait_recv()
        lax.fori_loop(c * PER_CHUNK, (c + 1) * PER_CHUNK, multiply(a_next), 0)
    seconds = [
        remote(
            second.at[pl.ds(lax.rem(r + d, reps) * share, share)], got_second.at[d],
            second_send.at[d], second_recv.at[d], (p_down, q, lax.rem(r + d, reps)),
        )
        for d in range(reps)
    ]
    for d in sorted(range(reps), key=lambda d: -min(d, reps - d)):
        there = lax.rem(r + d, reps)

        def keep_second(s, carry):
            keep(cw_next, second, there * share + s)
            return carry

        lax.fori_loop(0, share, keep_second, 0)
        seconds[d].start()

    total = first[pl.ds(r * share, share)]
    for d in range(1, reps):
        firsts[d - 1].wait_recv()
        total += got_first[d - 1]
    for d in range(reps):
        seconds[d].wait_recv()
        total += got_second[d]
    out[...] = total
    forwarded()
    for copy in small + panels + firsts + seconds:
        copy.wait_send()


def shards(rows, cols, reps, a_blocks, a_where, b_blocks, b_where, c_where):
    share = NC // reps
    a_spots = a_where.reshape(1, NA)
    b_spots = b_where.reshape(1, NB)
    c_spots = c_where.reshape(1, NC)
    smem, hbm, vmem = (pl.BlockSpec(memory_space=m) for m in (pltpu.SMEM, pl.ANY, pltpu.VMEM))
    dma = pltpu.SemaphoreType.DMA
    f32, i32, bf16 = jnp.float32, jnp.int32, jnp.bfloat16
    result = pl.pallas_call(
        functools.partial(kernel, rows, cols, reps),
        out_shape=jax.ShapeDtypeStruct((share, BLOCK, BLOCK), f32),
        in_specs=[smem, smem, smem, hbm, hbm, hbm, hbm],
        out_specs=vmem,
        scratch_shapes=[
            pltpu.VMEM((NA, BLOCK, BLOCK), f32),
            pltpu.VMEM((NB, BLOCK, BLOCK), f32),
            pltpu.VMEM((NA, BLOCK, BLOCK), f32),
            pltpu.VMEM((NA // 2, BLOCK, BLOCK), f32),
            pltpu.VMEM((1, NA), i32),
            pltpu.VMEM((1, NC), i32),
            pltpu.SMEM((1, NA), i32),
            pltpu.SMEM((1, NC), i32),
            pltpu.VMEM((KSET, 2 * BLOCK, CB * BLOCK), bf16),
            pltpu.VMEM((NA * CB, BLOCK, BLOCK), f32),
            pltpu.VMEM((NC, BLOCK, BLOCK), f32),
            pltpu.VMEM((NC, BLOCK, BLOCK), f32),
            pltpu.VMEM((max(reps - 1, 1), share, BLOCK, BLOCK), f32),
            pltpu.VMEM((reps, share, BLOCK, BLOCK), f32),
            pltpu.SMEM((NB,), i32),
            pltpu.SMEM((NA,), i32),
            pltpu.SMEM((NB,), i32),
            pltpu.SMEM((NA,), i32),
            dma((2,)), dma((2,)), dma((2,)), dma((2,)), dma((CHUNKS,)), dma((CHUNKS,)),
            dma((CHUNKS // 2,)), dma((CHUNKS // 2,)),
            dma((max(reps - 1, 1),)), dma((max(reps - 1, 1),)), dma((reps,)), dma((reps,)),
        ],
        compiler_params=pltpu.CompilerParams(
            collective_id=0, has_side_effects=True, vmem_limit_bytes=60 * 1024 * 1024
        ),
        cost_estimate=pl.CostEstimate(flops=2 * 2 * NA * 4 * CB * BLOCK**3, bytes_accessed=4 << 20, transcendentals=0),
    )(
        a_spots, b_spots, c_spots,
        a_blocks.reshape(NA, BLOCK, BLOCK), b_blocks.reshape(NB, BLOCK, BLOCK), a_spots, c_spots,
    )
    return result[None, None]


def solution(mesh):
    in_specs = (
        P("row", "col", "rep", None, None, None),
        P("row", "col", "rep", None),
        P("row", "col", "rep", None, None, None),
        P("row", "col", "rep", None),
        P("row", "col", None),
    )
    out_specs = P("row", "col", "rep", None, None)
    body = functools.partial(shards, mesh.shape["row"], mesh.shape["col"], mesh.shape["rep"])
    return jax.shard_map(body, mesh=mesh, in_specs=in_specs, out_specs=out_specs, check_vma=False)
```

```python
import functools

import jax
import jax.numpy as jnp
from jax import lax
from jax.experimental import pallas as pl
from jax.experimental.pallas import tpu as pltpu
from jax.sharding import PartitionSpec as P

KB = 64
CB = 4
RB = 4
KSET = 8
NA = 16
NB = 32
NC = 8
BLOCK = 128
CHUNKS = 8
PER_CHUNK = NA // CHUNKS
STRAIGHT = 2
WAYS = (((3,), 3), ((7,), 3))
RELAYED = (1, 2)
MESH = pl.DeviceIdType.MESH


def sort_order(where, count, rank, order):
    def rank_one(n, carry):
        mine = where[0, n]
        below = jnp.int32(0)
        for m in range(count):
            below += (where[0, m] < mine).astype(jnp.int32)
        rank[n] = below
        return carry

    lax.fori_loop(0, count, rank_one, 0)

    def place_one(t, carry):
        found = jnp.int32(0)
        for n in range(count):
            found = jnp.where(rank[n] == t, n, found)
        order[t] = found
        return carry

    lax.fori_loop(0, count, place_one, 0)


def split(x):
    high = x.astype(jnp.bfloat16)
    low = (x - high.astype(jnp.float32)).astype(jnp.bfloat16)
    return high, low


def kernel(
    rows, cols, reps,
    a_where, b_where, c_where, a_hbm, b_hbm, aw_hbm, cw_hbm, out,
    a_own, b_own, a_next, via, aw_land, cw_land, aw_next, cw_next, right, pieces, first, second, got_first, got_second, relay, relay_sum,
    rank, a_order, b_order, inner,
    local_sem, meta_sem, small_send, small_recv, a_send, a_recv, via_send, via_recv, first_send, first_recv, second_send, second_recv, relay_out, relay_recv, relay_send, relay_landed,
):
    p, q, r = lax.axis_index("row"), lax.axis_index("col"), lax.axis_index("rep")
    p_up, p_down = lax.rem(p + 1, rows), lax.rem(p + rows - 1, rows)
    q_up, q_down = lax.rem(q + 1, cols), lax.rem(q + cols - 1, cols)
    share = NC // reps

    load_a = pltpu.make_async_copy(a_hbm, a_own, local_sem.at[0])
    load_b = pltpu.make_async_copy(b_hbm, b_own, local_sem.at[1])
    load_b.start()
    load_a.start()

    width = rows // 2
    x, half = lax.rem(p, width), p // width
    last = width - 1
    ways, taken = [], STRAIGHT
    for stops, count in WAYS:
        ways.append((stops, taken, count))
        taken += count
    relayed = (r == RELAYED[0]) | (r == RELAYED[1])
    across = lax.rem(p + width, rows)

    def row_at(at, side):
        return side * width + at

    def remote(src, dst, send_sem, recv_sem, device):
        return pltpu.make_async_remote_copy(
            src_ref=src, dst_ref=dst, send_sem=send_sem, recv_sem=recv_sem, device_id=device, device_id_type=MESH
        )

    barrier = pltpu.get_barrier_semaphore()

    def greet(*device):
        pl.semaphore_signal(barrier, inc=1, device_id=device, device_id_type=MESH)

    greet(p_down, q_up, r)
    greet(p_down, q, r)
    for d in range(reps):
        there = lax.rem(r + d, reps)
        greet(p_up, q, there)
        if d:
            greet(p, q, there)

    far_side = 1 - half

    for stops, _, _ in ways:
        for n, place in enumerate(stops):
            @pl.when(x == place)
            def _():
                greet(row_at(stops[n - 1], half) if n else row_at(last, far_side), q, r)

    @pl.when(x == 0)
    def _():
        for stops, _, _ in ways:
            greet(row_at(stops[-1], half), q_up, r)

    @pl.when((x == 0) & relayed)
    def _():
        for d in range(reps):
            greet(across, q, lax.rem(r + d, reps))

    @pl.when((x == last) & relayed)
    def _():
        greet(row_at(0, half), q, r)

    more = jnp.where(x == last, len(ways), 0)
    for stops, _, _ in ways:
        for place in stops:
            more += jnp.where(x == place, 1, 0)
    more += jnp.where(x == 0, len(RELAYED), 0) + jnp.where((x == 0) & relayed, 1, 0)
    pl.semaphore_wait(barrier, 2 * reps + 1 + more)

    away = (p_up, q_down, r)
    small = [
        remote(aw_hbm, aw_land, small_send.at[0], small_recv.at[0], away),
        remote(cw_hbm, cw_land, small_send.at[1], small_recv.at[1], (p_up, q, r)),
    ]
    for copy in small:
        copy.start()

    def part(c):
        return pl.ds(c * PER_CHUNK, PER_CHUNK)

    panels = [
        remote(a_hbm.at[part(c)], a_next.at[part(c)], a_send.at[c], a_recv.at[c], away) for c in range(CHUNKS)
    ]

    def leg(c, at, device):
        return remote(a_hbm.at[part(c)], via.at[part(at)], a_send.at[c], via_recv.at[at], device)

    def pass_on(at, device):
        return remote(via.at[part(at)], via.at[part(at)], via_send.at[at], via_recv.at[at], device)

    def land(at, c):
        return remote(
            via.at[part(at)], a_next.at[part(c)], via_send.at[at], a_recv.at[c], (row_at(0, half), q_down, r)
        )

    @pl.when(x != last)
    def _():
        for copy in panels:
            copy.start()

    def send_around(at):
        @pl.when(x == last)
        def _():
            for stops, start, count in ways:
                if at < count:
                    leg(start + at, at, (row_at(stops[0], far_side), q, r)).start()
            if at < STRAIGHT:
                panels[at].start()

    send_around(0)

    def next_leg(n, stops, at, c):
        return pass_on(at, (row_at(stops[n + 1], half), q, r)) if n + 1 < len(stops) else land(at, c)

    def forward():
        for stops, start, count in ways:
            for n, place in enumerate(stops):
                @pl.when(x == place)
                def _():
                    for at in range(count):
                        pass_on(at, away).wait_recv()
                        next_leg(n, stops, at, start + at).start()

    def forwarded():
        for stops, start, count in ways:
            for n, place in enumerate(stops):
                @pl.when(x == place)
                def _():
                    for at in range(count):
                        next_leg(n, stops, at, start + at).wait_send()

    sort_order(b_where, NB, rank, b_order)
    load_b.wait()

    def lay_right(u, carry):
        for j in range(CB):
            high, low = split(b_own[b_order[u * CB + j]])
            at = slice(j * BLOCK, (j + 1) * BLOCK)
            right[u, :BLOCK, at] = high
            right[u, BLOCK:, at] = low
        return carry

    lax.fori_loop(0, KSET, lay_right, 0)
    send_around(1)

    def places(where):
        def one(n, carry):
            k = lax.rem(where[0, n], KB)
            slot = jnp.int32(0)
            for u in range(1, KSET):
                slot += (b_where[0, b_order[u * CB]] <= k * CB).astype(jnp.int32)
            inner[n] = slot
            return carry

        lax.fori_loop(0, NA, one, 0)
        sort_order(where, NA, rank, a_order)

    def multiply(blocks):
        def one(n, carry):
            high, low = split(blocks[n])
            left = jnp.concatenate(
                [jnp.concatenate([high, high], axis=1), jnp.concatenate([low, low], axis=1)], axis=0
            )
            both = jnp.dot(left, right[inner[n]], preferred_element_type=jnp.float32)
            total = both[:BLOCK] + both[BLOCK:]
            for j in range(CB):
                pieces[n * CB + j] = total[:, j * BLOCK:(j + 1) * BLOCK]
            return carry

        return one

    def keep(spots, into, s):
        spot = spots[0, s]
        i, j = spot // CB, lax.rem(spot, CB)
        total = pieces[a_order[i * RB] * CB + j]
        for t in range(1, RB):
            total += pieces[a_order[i * RB + t] * CB + j]
        into[s] = total

    places(a_where)
    load_a.wait()
    lax.fori_loop(0, NA // 2, multiply(a_own), 0)
    send_around(2)
    lax.fori_loop(NA // 2, NA, multiply(a_own), 0)

    def keep_first(s, carry):
        keep(c_where, first, s)
        return carry

    lax.fori_loop(0, NC, keep_first, 0)
    firsts = [
        remote(
            first.at[pl.ds(lax.rem(r + d, reps) * share, share)], got_first.at[d - 1],
            first_send.at[d - 1], first_recv.at[d - 1], (p, q, lax.rem(r + d, reps)),
        )
        for d in range(1, reps)
    ]
    forward()

    @pl.when(x != 0)
    def _():
        for copy in firsts:
            copy.start()

    for copy in small:
        copy.wait_recv()
    to_scalars = [
        pltpu.make_async_copy(aw_land, aw_next, meta_sem.at[0]),
        pltpu.make_async_copy(cw_land, cw_next, meta_sem.at[1]),
    ]
    for copy in to_scalars:
        copy.start()
    for copy in to_scalars:
        copy.wait()
    places(aw_next)
    for c in range(CHUNKS):
        panels[c].wait_recv()
        lax.fori_loop(c * PER_CHUNK, (c + 1) * PER_CHUNK, multiply(a_next), 0)
        if c == STRAIGHT - 1:
            @pl.when(x == 0)
            def _():
                for copy in firsts:
                    copy.start()
    def straight_back(d, count):
        return remote(
            second.at[pl.ds(lax.rem(r + d, reps) * share, count)], got_second.at[d, pl.ds(0, count)],
            second_send.at[d], second_recv.at[d], (p_down, q, lax.rem(r + d, reps)),
        )

    def to_relay(d):
        return remote(
            second.at[pl.ds(lax.rem(r + d, reps) * share + share - 1, 1)], relay.at[d],
            relay_out.at[d], relay_recv.at[d], (across, q, lax.rem(r + d, reps)),
        )

    def turned(d):
        there = lax.rem(r + d, reps)
        return (x == 0) & ((there == RELAYED[0]) | (there == RELAYED[1]))

    relay_on = remote(
        relay_sum, got_second.at[0, pl.ds(share - 1, 1)], relay_send, relay_landed, (row_at(0, half) + last, q, r)
    )
    for d in sorted(range(reps), key=lambda d: -min(d, reps - d)):
        there = lax.rem(r + d, reps)
        def keep_second(s, carry):
            keep(cw_next, second, there * share + s)
            return carry

        lax.fori_loop(0, share, keep_second, 0)

        @pl.when(turned(d))
        def _():
            to_relay(d).start()
            straight_back(d, share - 1).start()

        @pl.when(jnp.logical_not(turned(d)))
        def _():
            straight_back(d, share).start()

    @pl.when((x == 0) & relayed)
    def _():
        to_relay(0).wait_recv()
        relay_sum[...] = relay[0]
        for d in range(1, reps):
            to_relay(d).wait_recv()
            relay_sum[...] += relay[d]
        relay_on.start()

    out[...] = first[pl.ds(r * share, share)]
    for d in range(1, reps):
        firsts[d - 1].wait_recv()
        out[...] += got_first[d - 1]

    @pl.when((x == last) & relayed)
    def _():
        for d in range(reps):
            straight_back(d, share - 1).wait_recv()
            out[:share - 1] += got_second[d, :share - 1]
        relay_on.wait_recv()
        out[share - 1:] += got_second[0, share - 1:]

    @pl.when(jnp.logical_not((x == last) & relayed))
    def _():
        for d in range(reps):
            straight_back(d, share).wait_recv()
            out[...] += got_second[d]

    @pl.when((x == 0) & relayed)
    def _():
        relay_on.wait_send()

    for d in range(reps):
        @pl.when(turned(d))
        def _():
            to_relay(d).wait_send()
            straight_back(d, share - 1).wait_send()

        @pl.when(jnp.logical_not(turned(d)))
        def _():
            straight_back(d, share).wait_send()

    forwarded()
    for copy in small + panels + firsts:
        copy.wait_send()


def shards(rows, cols, reps, a_blocks, a_where, b_blocks, b_where, c_where):
    share = NC // reps
    a_spots = a_where.reshape(1, NA)
    b_spots = b_where.reshape(1, NB)
    c_spots = c_where.reshape(1, NC)
    smem, hbm, vmem = (pl.BlockSpec(memory_space=m) for m in (pltpu.SMEM, pl.ANY, pltpu.VMEM))
    dma = pltpu.SemaphoreType.DMA
    f32, i32, bf16 = jnp.float32, jnp.int32, jnp.bfloat16
    result = pl.pallas_call(
        functools.partial(kernel, rows, cols, reps),
        out_shape=jax.ShapeDtypeStruct((share, BLOCK, BLOCK), f32),
        in_specs=[smem, smem, smem, hbm, hbm, hbm, hbm],
        out_specs=vmem,
        scratch_shapes=[
            pltpu.VMEM((NA, BLOCK, BLOCK), f32),
            pltpu.VMEM((NB, BLOCK, BLOCK), f32),
            pltpu.VMEM((NA, BLOCK, BLOCK), f32),
            pltpu.VMEM((max(count for _, count in WAYS) * PER_CHUNK, BLOCK, BLOCK), f32),
            pltpu.VMEM((1, NA), i32),
            pltpu.VMEM((1, NC), i32),
            pltpu.SMEM((1, NA), i32),
            pltpu.SMEM((1, NC), i32),
            pltpu.VMEM((KSET, 2 * BLOCK, CB * BLOCK), bf16),
            pltpu.VMEM((NA * CB, BLOCK, BLOCK), f32),
            pltpu.VMEM((NC, BLOCK, BLOCK), f32),
            pltpu.VMEM((NC, BLOCK, BLOCK), f32),
            pltpu.VMEM((max(reps - 1, 1), share, BLOCK, BLOCK), f32),
            pltpu.VMEM((reps, share, BLOCK, BLOCK), f32),
            pltpu.VMEM((reps, 1, BLOCK, BLOCK), f32),
            pltpu.VMEM((1, BLOCK, BLOCK), f32),
            pltpu.SMEM((NB,), i32),
            pltpu.SMEM((NA,), i32),
            pltpu.SMEM((NB,), i32),
            pltpu.SMEM((NA,), i32),
            dma((2,)), dma((2,)), dma((2,)), dma((2,)), dma((CHUNKS,)), dma((CHUNKS,)),
            dma((max(count for _, count in WAYS),)), dma((max(count for _, count in WAYS),)),
            dma((max(reps - 1, 1),)), dma((max(reps - 1, 1),)), dma((reps,)), dma((reps,)), dma((reps,)), dma((reps,)), dma, dma,
        ],
        compiler_params=pltpu.CompilerParams(
            collective_id=0, has_side_effects=True, vmem_limit_bytes=60 * 1024 * 1024
        ),
        cost_estimate=pl.CostEstimate(flops=2 * 2 * NA * 4 * CB * BLOCK**3, bytes_accessed=4 << 20, transcendentals=0),
    )(
        a_spots, b_spots, c_spots,
        a_blocks.reshape(NA, BLOCK, BLOCK), b_blocks.reshape(NB, BLOCK, BLOCK), a_spots, c_spots,
    )
    return result[None, None]


def solution(mesh):
    in_specs = (
        P("row", "col", "rep", None, None, None),
        P("row", "col", "rep", None),
        P("row", "col", "rep", None, None, None),
        P("row", "col", "rep", None),
        P("row", "col", None),
    )
    out_specs = P("row", "col", "rep", None, None)
    body = functools.partial(shards, mesh.shape["row"], mesh.shape["col"], mesh.shape["rep"])
    return jax.shard_map(body, mesh=mesh, in_specs=in_specs, out_specs=out_specs, check_vma=False)
```

```python
import functools

import jax
import jax.numpy as jnp
from jax import lax
from jax.experimental import pallas as pl
from jax.experimental.pallas import tpu as pltpu
from jax.sharding import PartitionSpec as P

KB = 64
CB = 4
RB = 4
KSET = 8
NA = 16
NB = 32
NC = 8
BLOCK = 128
CHUNKS = 8
PER_CHUNK = NA // CHUNKS
STRAIGHT = 2
WAYS = (((7,), 3), ((3,), 3))
RELAYED = (1, 2)
MESH = pl.DeviceIdType.MESH


def sort_order(where, count, rank, order):
    def rank_one(n, carry):
        mine = where[0, n]
        below = jnp.int32(0)
        for m in range(count):
            below += (where[0, m] < mine).astype(jnp.int32)
        rank[n] = below
        return carry

    lax.fori_loop(0, count, rank_one, 0)

    def place_one(t, carry):
        found = jnp.int32(0)
        for n in range(count):
            found = jnp.where(rank[n] == t, n, found)
        order[t] = found
        return carry

    lax.fori_loop(0, count, place_one, 0)


def split(x):
    high = x.astype(jnp.bfloat16)
    low = (x - high.astype(jnp.float32)).astype(jnp.bfloat16)
    return high, low


def kernel(
    rows, cols, reps,
    a_where, b_where, c_where, a_hbm, b_hbm, aw_hbm, cw_hbm, out,
    a_own, b_own, a_next, via, aw_land, cw_land, aw_next, cw_next, right, pieces, first, second, got_first, got_second, relay, relay_sum,
    rank, a_order, b_order, inner,
    local_sem, meta_sem, small_send, small_recv, a_send, a_recv, via_send, via_recv, first_send, first_recv, second_send, second_recv, relay_out, relay_recv, relay_send, relay_landed,
):
    p, q, r = lax.axis_index("row"), lax.axis_index("col"), lax.axis_index("rep")
    p_up, p_down = lax.rem(p + 1, rows), lax.rem(p + rows - 1, rows)
    q_up, q_down = lax.rem(q + 1, cols), lax.rem(q + cols - 1, cols)
    share = NC // reps

    load_a = pltpu.make_async_copy(a_hbm, a_own, local_sem.at[0])
    load_b = pltpu.make_async_copy(b_hbm, b_own, local_sem.at[1])
    load_b.start()
    load_a.start()

    width = rows // 2
    x, half = lax.rem(p, width), p // width
    last = width - 1
    ways, taken = [], STRAIGHT
    for stops, count in WAYS:
        ways.append((stops, taken, count))
        taken += count
    beside = last - 1

    def is_relayed(rep):
        return functools.reduce(jnp.logical_or, [rep == one for one in RELAYED])

    relayed = is_relayed(r)
    relaying = ((x == 0) & relayed) | ((x == beside) & jnp.logical_not(relayed))
    across = lax.rem(p + width, rows)

    def row_at(at, side):
        return side * width + at

    def remote(src, dst, send_sem, recv_sem, device):
        return pltpu.make_async_remote_copy(
            src_ref=src, dst_ref=dst, send_sem=send_sem, recv_sem=recv_sem, device_id=device, device_id_type=MESH
        )

    barrier = pltpu.get_barrier_semaphore()

    def greet(*device):
        pl.semaphore_signal(barrier, inc=1, device_id=device, device_id_type=MESH)

    greet(p_down, q_up, r)
    greet(p_down, q, r)
    for d in range(reps):
        there = lax.rem(r + d, reps)
        greet(p_up, q, there)
        if d:
            greet(p, q, there)

    far_side = 1 - half

    for stops, _, _ in ways:
        for n, place in enumerate(stops):
            @pl.when(x == place)
            def _():
                greet(row_at(stops[n - 1], half) if n else row_at(last, far_side), q, r)

    @pl.when(x == 0)
    def _():
        for stops, _, _ in ways:
            greet(row_at(stops[-1], half), q_up, r)

    @pl.when(relaying)
    def _():
        for d in range(reps):
            greet(row_at(0, far_side), q, lax.rem(r + d, reps))

    @pl.when(x == last)
    def _():
        greet(row_at(jnp.where(relayed, 0, beside), half), q, r)

    more = jnp.where(x == last, len(ways), 0)
    for stops, _, _ in ways:
        for place in stops:
            more += jnp.where(x == place, 1, 0)
    more += jnp.where(x == 0, reps, 0) + jnp.where(relaying, 1, 0)
    pl.semaphore_wait(barrier, 2 * reps + 1 + more)

    away = (p_up, q_down, r)
    small = [
        remote(aw_hbm, aw_land, small_send.at[0], small_recv.at[0], away),
        remote(cw_hbm, cw_land, small_send.at[1], small_recv.at[1], (p_up, q, r)),
    ]
    for copy in small:
        copy.start()

    def part(c):
        return pl.ds(c * PER_CHUNK, PER_CHUNK)

    panels = [
        remote(a_hbm.at[part(c)], a_next.at[part(c)], a_send.at[c], a_recv.at[c], away) for c in range(CHUNKS)
    ]

    def leg(c, at, device):
        return remote(a_hbm.at[part(c)], via.at[part(at)], a_send.at[c], via_recv.at[at], device)

    def pass_on(at, device):
        return remote(via.at[part(at)], via.at[part(at)], via_send.at[at], via_recv.at[at], device)

    def land(at, c):
        return remote(
            via.at[part(at)], a_next.at[part(c)], via_send.at[at], a_recv.at[c], (row_at(0, half), q_down, r)
        )

    @pl.when(x != last)
    def _():
        for copy in panels:
            copy.start()

    def send_around(at):
        @pl.when(x == last)
        def _():
            for stops, start, count in ways:
                if at < count:
                    leg(start + at, at, (row_at(stops[0], far_side), q, r)).start()
            if at < STRAIGHT:
                panels[at].start()

    send_around(0)

    def next_leg(n, stops, at, c):
        return pass_on(at, (row_at(stops[n + 1], half), q, r)) if n + 1 < len(stops) else land(at, c)

    def forward():
        for stops, start, count in ways:
            for n, place in enumerate(stops):
                @pl.when(x == place)
                def _():
                    for at in range(count):
                        pass_on(at, away).wait_recv()
                        next_leg(n, stops, at, start + at).start()

    def forwarded():
        for stops, start, count in ways:
            for n, place in enumerate(stops):
                @pl.when(x == place)
                def _():
                    for at in range(count):
                        next_leg(n, stops, at, start + at).wait_send()

    sort_order(b_where, NB, rank, b_order)
    load_b.wait()

    def lay_right(u, carry):
        for j in range(CB):
            high, low = split(b_own[b_order[u * CB + j]])
            at = slice(j * BLOCK, (j + 1) * BLOCK)
            right[u, :BLOCK, at] = high
            right[u, BLOCK:, at] = low
        return carry

    lax.fori_loop(0, KSET, lay_right, 0)
    send_around(1)

    def places(where):
        def one(n, carry):
            k = lax.rem(where[0, n], KB)
            slot = jnp.int32(0)
            for u in range(1, KSET):
                slot += (b_where[0, b_order[u * CB]] <= k * CB).astype(jnp.int32)
            inner[n] = slot
            return carry

        lax.fori_loop(0, NA, one, 0)
        sort_order(where, NA, rank, a_order)

    def multiply(blocks):
        def one(n, carry):
            high, low = split(blocks[n])
            left = jnp.concatenate(
                [jnp.concatenate([high, high], axis=1), jnp.concatenate([low, low], axis=1)], axis=0
            )
            both = jnp.dot(left, right[inner[n]], preferred_element_type=jnp.float32)
            total = both[:BLOCK] + both[BLOCK:]
            for j in range(CB):
                pieces[n * CB + j] = total[:, j * BLOCK:(j + 1) * BLOCK]
            return carry

        return one

    def keep(spots, into, s):
        spot = spots[0, s]
        i, j = spot // CB, lax.rem(spot, CB)
        total = pieces[a_order[i * RB] * CB + j]
        for t in range(1, RB):
            total += pieces[a_order[i * RB + t] * CB + j]
        into[s] = total

    places(a_where)
    load_a.wait()
    lax.fori_loop(0, NA // 2, multiply(a_own), 0)
    send_around(2)
    lax.fori_loop(NA // 2, NA, multiply(a_own), 0)

    def keep_first(s, carry):
        keep(c_where, first, s)
        return carry

    lax.fori_loop(0, NC, keep_first, 0)
    firsts = [
        remote(
            first.at[pl.ds(lax.rem(r + d, reps) * share, share)], got_first.at[d - 1],
            first_send.at[d - 1], first_recv.at[d - 1], (p, q, lax.rem(r + d, reps)),
        )
        for d in range(1, reps)
    ]
    forward()

    @pl.when(x != 0)
    def _():
        for copy in firsts:
            copy.start()

    for copy in small:
        copy.wait_recv()
    to_scalars = [
        pltpu.make_async_copy(aw_land, aw_next, meta_sem.at[0]),
        pltpu.make_async_copy(cw_land, cw_next, meta_sem.at[1]),
    ]
    for copy in to_scalars:
        copy.start()
    for copy in to_scalars:
        copy.wait()
    places(aw_next)
    for c in range(CHUNKS):
        panels[c].wait_recv()
        lax.fori_loop(c * PER_CHUNK, (c + 1) * PER_CHUNK, multiply(a_next), 0)
        if c == STRAIGHT - 1:
            @pl.when(x == 0)
            def _():
                for copy in firsts:
                    copy.start()
    def straight_back(d, count):
        return remote(
            second.at[pl.ds(lax.rem(r + d, reps) * share, count)], got_second.at[d, pl.ds(0, count)],
            second_send.at[d], second_recv.at[d], (p_down, q, lax.rem(r + d, reps)),
        )

    def to_relay(d):
        there = lax.rem(r + d, reps)
        return remote(
            second.at[pl.ds(there * share + share - 1, 1)], relay.at[d], relay_out.at[d], relay_recv.at[d],
            (row_at(jnp.where(is_relayed(there), 0, beside), far_side), q, there),
        )

    relay_on = remote(
        relay_sum, got_second.at[0, pl.ds(share - 1, 1)], relay_send, relay_landed, (row_at(last, half), q, r)
    )
    for d in sorted(range(reps), key=lambda d: -min(d, reps - d)):
        there = lax.rem(r + d, reps)
        def keep_second(s, carry):
            keep(cw_next, second, there * share + s)
            return carry

        lax.fori_loop(0, share, keep_second, 0)

        @pl.when(x == 0)
        def _():
            to_relay(d).start()
            straight_back(d, share - 1).start()

        @pl.when(x != 0)
        def _():
            straight_back(d, share).start()

    @pl.when(relaying)
    def _():
        to_relay(0).wait_recv()
        relay_sum[...] = relay[0]
        for d in range(1, reps):
            to_relay(d).wait_recv()
            relay_sum[...] += relay[d]
        relay_on.start()

    out[...] = first[pl.ds(r * share, share)]
    for d in range(1, reps):
        firsts[d - 1].wait_recv()
        out[...] += got_first[d - 1]

    @pl.when(x == last)
    def _():
        for d in range(reps):
            straight_back(d, share - 1).wait_recv()
            out[:share - 1] += got_second[d, :share - 1]
        relay_on.wait_recv()
        out[share - 1:] += got_second[0, share - 1:]

    @pl.when(x != last)
    def _():
        for d in range(reps):
            straight_back(d, share).wait_recv()
            out[...] += got_second[d]

    @pl.when(relaying)
    def _():
        relay_on.wait_send()

    for d in range(reps):
        @pl.when(x == 0)
        def _():
            to_relay(d).wait_send()
            straight_back(d, share - 1).wait_send()

        @pl.when(x != 0)
        def _():
            straight_back(d, share).wait_send()

    forwarded()
    for copy in small + panels + firsts:
        copy.wait_send()


def shards(rows, cols, reps, a_blocks, a_where, b_blocks, b_where, c_where):
    share = NC // reps
    a_spots = a_where.reshape(1, NA)
    b_spots = b_where.reshape(1, NB)
    c_spots = c_where.reshape(1, NC)
    smem, hbm, vmem = (pl.BlockSpec(memory_space=m) for m in (pltpu.SMEM, pl.ANY, pltpu.VMEM))
    dma = pltpu.SemaphoreType.DMA
    f32, i32, bf16 = jnp.float32, jnp.int32, jnp.bfloat16
    result = pl.pallas_call(
        functools.partial(kernel, rows, cols, reps),
        out_shape=jax.ShapeDtypeStruct((share, BLOCK, BLOCK), f32),
        in_specs=[smem, smem, smem, hbm, hbm, hbm, hbm],
        out_specs=vmem,
        scratch_shapes=[
            pltpu.VMEM((NA, BLOCK, BLOCK), f32),
            pltpu.VMEM((NB, BLOCK, BLOCK), f32),
            pltpu.VMEM((NA, BLOCK, BLOCK), f32),
            pltpu.VMEM((max(count for _, count in WAYS) * PER_CHUNK, BLOCK, BLOCK), f32),
            pltpu.VMEM((1, NA), i32),
            pltpu.VMEM((1, NC), i32),
            pltpu.SMEM((1, NA), i32),
            pltpu.SMEM((1, NC), i32),
            pltpu.VMEM((KSET, 2 * BLOCK, CB * BLOCK), bf16),
            pltpu.VMEM((NA * CB, BLOCK, BLOCK), f32),
            pltpu.VMEM((NC, BLOCK, BLOCK), f32),
            pltpu.VMEM((NC, BLOCK, BLOCK), f32),
            pltpu.VMEM((max(reps - 1, 1), share, BLOCK, BLOCK), f32),
            pltpu.VMEM((reps, share, BLOCK, BLOCK), f32),
            pltpu.VMEM((reps, 1, BLOCK, BLOCK), f32),
            pltpu.VMEM((1, BLOCK, BLOCK), f32),
            pltpu.SMEM((NB,), i32),
            pltpu.SMEM((NA,), i32),
            pltpu.SMEM((NB,), i32),
            pltpu.SMEM((NA,), i32),
            dma((2,)), dma((2,)), dma((2,)), dma((2,)), dma((CHUNKS,)), dma((CHUNKS,)),
            dma((max(count for _, count in WAYS),)), dma((max(count for _, count in WAYS),)),
            dma((max(reps - 1, 1),)), dma((max(reps - 1, 1),)), dma((reps,)), dma((reps,)), dma((reps,)), dma((reps,)), dma, dma,
        ],
        compiler_params=pltpu.CompilerParams(
            collective_id=0, has_side_effects=True, vmem_limit_bytes=60 * 1024 * 1024
        ),
        cost_estimate=pl.CostEstimate(flops=2 * 2 * NA * 4 * CB * BLOCK**3, bytes_accessed=4 << 20, transcendentals=0),
    )(
        a_spots, b_spots, c_spots,
        a_blocks.reshape(NA, BLOCK, BLOCK), b_blocks.reshape(NB, BLOCK, BLOCK), a_spots, c_spots,
    )
    return result[None, None]


def solution(mesh):
    in_specs = (
        P("row", "col", "rep", None, None, None),
        P("row", "col", "rep", None),
        P("row", "col", "rep", None, None, None),
        P("row", "col", "rep", None),
        P("row", "col", None),
    )
    out_specs = P("row", "col", "rep", None, None)
    body = functools.partial(shards, mesh.shape["row"], mesh.shape["col"], mesh.shape["rep"])
    return jax.shard_map(body, mesh=mesh, in_specs=in_specs, out_specs=out_specs, check_vma=False)
```

```python
import functools

import jax
import jax.numpy as jnp
from jax import lax
from jax.experimental import pallas as pl
from jax.experimental.pallas import tpu as pltpu
from jax.sharding import PartitionSpec as P

KB = 64
CB = 4
RB = 4
KSET = 8
NA = 16
NB = 32
NC = 8
BLOCK = 128
CHUNKS = 16
PER_CHUNK = NA // CHUNKS
STRAIGHT = 5
WAYS = (((7,), 6), ((3,), 5))
RELAYED = (1,)
MESH = pl.DeviceIdType.MESH


def sort_order(where, count, rank, order):
    def rank_one(n, carry):
        mine = where[0, n]
        below = jnp.int32(0)
        for m in range(count):
            below += (where[0, m] < mine).astype(jnp.int32)
        rank[n] = below
        return carry

    lax.fori_loop(0, count, rank_one, 0)

    def place_one(t, carry):
        found = jnp.int32(0)
        for n in range(count):
            found = jnp.where(rank[n] == t, n, found)
        order[t] = found
        return carry

    lax.fori_loop(0, count, place_one, 0)


def split(x):
    high = x.astype(jnp.bfloat16)
    low = (x - high.astype(jnp.float32)).astype(jnp.bfloat16)
    return high, low


def kernel(
    rows, cols, reps,
    a_where, b_where, c_where, a_hbm, b_hbm, aw_hbm, cw_hbm, out,
    a_own, b_own, a_next, via, aw_land, cw_land, aw_next, cw_next, right, pieces, first, second, got_first, got_second, relay, relay_sum,
    rank, a_order, b_order, inner,
    local_sem, meta_sem, small_send, small_recv, a_send, a_recv, via_send, via_recv, first_send, first_recv, second_send, second_recv, relay_out, relay_recv, relay_send, relay_landed,
):
    p, q, r = lax.axis_index("row"), lax.axis_index("col"), lax.axis_index("rep")
    p_up, p_down = lax.rem(p + 1, rows), lax.rem(p + rows - 1, rows)
    q_up, q_down = lax.rem(q + 1, cols), lax.rem(q + cols - 1, cols)
    share = NC // reps

    load_a = pltpu.make_async_copy(a_hbm, a_own, local_sem.at[0])
    load_b = pltpu.make_async_copy(b_hbm, b_own, local_sem.at[1])
    load_b.start()
    load_a.start()

    width = rows // 2
    x, half = lax.rem(p, width), p // width
    last = width - 1
    ways, taken = [], STRAIGHT
    for stops, count in WAYS:
        ways.append((stops, taken, count))
        taken += count
    beside = last - 1

    def is_relayed(rep):
        return functools.reduce(jnp.logical_or, [rep == one for one in RELAYED])

    relayed = is_relayed(r)
    relaying = ((x == 0) & relayed) | ((x == beside) & jnp.logical_not(relayed))
    across = lax.rem(p + width, rows)

    def row_at(at, side):
        return side * width + at

    def remote(src, dst, send_sem, recv_sem, device):
        return pltpu.make_async_remote_copy(
            src_ref=src, dst_ref=dst, send_sem=send_sem, recv_sem=recv_sem, device_id=device, device_id_type=MESH
        )

    barrier = pltpu.get_barrier_semaphore()

    def greet(*device):
        pl.semaphore_signal(barrier, inc=1, device_id=device, device_id_type=MESH)

    greet(p_down, q_up, r)
    greet(p_down, q, r)
    for d in range(reps):
        there = lax.rem(r + d, reps)
        greet(p_up, q, there)
        if d:
            greet(p, q, there)

    far_side = 1 - half

    for stops, _, _ in ways:
        for n, place in enumerate(stops):
            @pl.when(x == place)
            def _():
                greet(row_at(stops[n - 1], half) if n else row_at(last, far_side), q, r)

    @pl.when(x == 0)
    def _():
        for stops, _, _ in ways:
            greet(row_at(stops[-1], half), q_up, r)

    @pl.when(relaying)
    def _():
        for d in range(reps):
            greet(row_at(0, far_side), q, lax.rem(r + d, reps))

    @pl.when(x == last)
    def _():
        greet(row_at(jnp.where(relayed, 0, beside), half), q, r)

    more = jnp.where(x == last, len(ways), 0)
    for stops, _, _ in ways:
        for place in stops:
            more += jnp.where(x == place, 1, 0)
    more += jnp.where(x == 0, reps, 0) + jnp.where(relaying, 1, 0)
    pl.semaphore_wait(barrier, 2 * reps + 1 + more)

    away = (p_up, q_down, r)
    small = [
        remote(aw_hbm, aw_land, small_send.at[0], small_recv.at[0], away),
        remote(cw_hbm, cw_land, small_send.at[1], small_recv.at[1], (p_up, q, r)),
    ]
    for copy in small:
        copy.start()

    def part(c):
        return pl.ds(c * PER_CHUNK, PER_CHUNK)

    panels = [
        remote(a_hbm.at[part(c)], a_next.at[part(c)], a_send.at[c], a_recv.at[c], away) for c in range(CHUNKS)
    ]

    def leg(c, at, device):
        return remote(a_hbm.at[part(c)], via.at[part(at)], a_send.at[c], via_recv.at[at], device)

    def pass_on(at, device):
        return remote(via.at[part(at)], via.at[part(at)], via_send.at[at], via_recv.at[at], device)

    def land(at, c):
        return remote(
            via.at[part(at)], a_next.at[part(c)], via_send.at[at], a_recv.at[c], (row_at(0, half), q_down, r)
        )

    @pl.when(x != last)
    def _():
        for copy in panels:
            copy.start()

    def send_around(turn):
        @pl.when(x == last)
        def _():
            for at in range(2 * turn, 2 * turn + 2):
                for stops, start, count in ways:
                    if at < count:
                        leg(start + at, at, (row_at(stops[0], far_side), q, r)).start()
                if at < STRAIGHT:
                    panels[at].start()

    send_around(0)

    def next_leg(n, stops, at, c):
        return pass_on(at, (row_at(stops[n + 1], half), q, r)) if n + 1 < len(stops) else land(at, c)

    def forward():
        for stops, start, count in ways:
            for n, place in enumerate(stops):
                @pl.when(x == place)
                def _():
                    for at in range(count):
                        pass_on(at, away).wait_recv()
                        next_leg(n, stops, at, start + at).start()

    def forwarded():
        for stops, start, count in ways:
            for n, place in enumerate(stops):
                @pl.when(x == place)
                def _():
                    for at in range(count):
                        next_leg(n, stops, at, start + at).wait_send()

    sort_order(b_where, NB, rank, b_order)
    load_b.wait()

    def lay_right(u, carry):
        for j in range(CB):
            high, low = split(b_own[b_order[u * CB + j]])
            at = slice(j * BLOCK, (j + 1) * BLOCK)
            right[u, :BLOCK, at] = high
            right[u, BLOCK:, at] = low
        return carry

    lax.fori_loop(0, KSET, lay_right, 0)
    send_around(1)

    def places(where):
        def one(n, carry):
            k = lax.rem(where[0, n], KB)
            slot = jnp.int32(0)
            for u in range(1, KSET):
                slot += (b_where[0, b_order[u * CB]] <= k * CB).astype(jnp.int32)
            inner[n] = slot
            return carry

        lax.fori_loop(0, NA, one, 0)
        sort_order(where, NA, rank, a_order)

    def multiply(blocks):
        def one(n, carry):
            high, low = split(blocks[n])
            left = jnp.concatenate(
                [jnp.concatenate([high, high], axis=1), jnp.concatenate([low, low], axis=1)], axis=0
            )
            both = jnp.dot(left, right[inner[n]], preferred_element_type=jnp.float32)
            total = both[:BLOCK] + both[BLOCK:]
            for j in range(CB):
                pieces[n * CB + j] = total[:, j * BLOCK:(j + 1) * BLOCK]
            return carry

        return one

    def keep(spots, into, s):
        spot = spots[0, s]
        i, j = spot // CB, lax.rem(spot, CB)
        total = pieces[a_order[i * RB] * CB + j]
        for t in range(1, RB):
            total += pieces[a_order[i * RB + t] * CB + j]
        into[s] = total

    places(a_where)
    load_a.wait()
    lax.fori_loop(0, NA // 2, multiply(a_own), 0)
    send_around(2)
    lax.fori_loop(NA // 2, NA, multiply(a_own), 0)

    def keep_first(s, carry):
        keep(c_where, first, s)
        return carry

    lax.fori_loop(0, NC, keep_first, 0)
    firsts = [
        remote(
            first.at[pl.ds(lax.rem(r + d, reps) * share, share)], got_first.at[d - 1],
            first_send.at[d - 1], first_recv.at[d - 1], (p, q, lax.rem(r + d, reps)),
        )
        for d in range(1, reps)
    ]
    forward()

    @pl.when(x != 0)
    def _():
        for copy in firsts:
            copy.start()

    for copy in small:
        copy.wait_recv()
    to_scalars = [
        pltpu.make_async_copy(aw_land, aw_next, meta_sem.at[0]),
        pltpu.make_async_copy(cw_land, cw_next, meta_sem.at[1]),
    ]
    for copy in to_scalars:
        copy.start()
    for copy in to_scalars:
        copy.wait()
    places(aw_next)
    for c in range(CHUNKS):
        panels[c].wait_recv()
        lax.fori_loop(c * PER_CHUNK, (c + 1) * PER_CHUNK, multiply(a_next), 0)
        if c == STRAIGHT - 1:
            @pl.when(x == 0)
            def _():
                for copy in firsts:
                    copy.start()
    def straight_back(d, count):
        return remote(
            second.at[pl.ds(lax.rem(r + d, reps) * share, count)], got_second.at[d, pl.ds(0, count)],
            second_send.at[d], second_recv.at[d], (p_down, q, lax.rem(r + d, reps)),
        )

    def to_relay(d):
        there = lax.rem(r + d, reps)
        return remote(
            second.at[pl.ds(there * share + share - 1, 1)], relay.at[d], relay_out.at[d], relay_recv.at[d],
            (row_at(jnp.where(is_relayed(there), 0, beside), far_side), q, there),
        )

    relay_on = remote(
        relay_sum, got_second.at[0, pl.ds(share - 1, 1)], relay_send, relay_landed, (row_at(last, half), q, r)
    )
    for d in sorted(range(reps), key=lambda d: -min(d, reps - d)):
        there = lax.rem(r + d, reps)
        def keep_second(s, carry):
            keep(cw_next, second, there * share + s)
            return carry

        lax.fori_loop(0, share, keep_second, 0)

        @pl.when(x == 0)
        def _():
            to_relay(d).start()
            straight_back(d, share - 1).start()

        @pl.when(x != 0)
        def _():
            straight_back(d, share).start()

    @pl.when(relaying)
    def _():
        to_relay(0).wait_recv()
        relay_sum[...] = relay[0]
        for d in range(1, reps):
            to_relay(d).wait_recv()
            relay_sum[...] += relay[d]
        relay_on.start()

    out[...] = first[pl.ds(r * share, share)]
    for d in range(1, reps):
        firsts[d - 1].wait_recv()
        out[...] += got_first[d - 1]

    @pl.when(x == last)
    def _():
        for d in range(reps):
            straight_back(d, share - 1).wait_recv()
            out[:share - 1] += got_second[d, :share - 1]
        relay_on.wait_recv()
        out[share - 1:] += got_second[0, share - 1:]

    @pl.when(x != last)
    def _():
        for d in range(reps):
            straight_back(d, share).wait_recv()
            out[...] += got_second[d]

    @pl.when(relaying)
    def _():
        relay_on.wait_send()

    for d in range(reps):
        @pl.when(x == 0)
        def _():
            to_relay(d).wait_send()
            straight_back(d, share - 1).wait_send()

        @pl.when(x != 0)
        def _():
            straight_back(d, share).wait_send()

    forwarded()
    for copy in small + panels + firsts:
        copy.wait_send()


def shards(rows, cols, reps, a_blocks, a_where, b_blocks, b_where, c_where):
    share = NC // reps
    a_spots = a_where.reshape(1, NA)
    b_spots = b_where.reshape(1, NB)
    c_spots = c_where.reshape(1, NC)
    smem, hbm, vmem = (pl.BlockSpec(memory_space=m) for m in (pltpu.SMEM, pl.ANY, pltpu.VMEM))
    dma = pltpu.SemaphoreType.DMA
    f32, i32, bf16 = jnp.float32, jnp.int32, jnp.bfloat16
    result = pl.pallas_call(
        functools.partial(kernel, rows, cols, reps),
        out_shape=jax.ShapeDtypeStruct((share, BLOCK, BLOCK), f32),
        in_specs=[smem, smem, smem, hbm, hbm, hbm, hbm],
        out_specs=vmem,
        scratch_shapes=[
            pltpu.VMEM((NA, BLOCK, BLOCK), f32),
            pltpu.VMEM((NB, BLOCK, BLOCK), f32),
            pltpu.VMEM((NA, BLOCK, BLOCK), f32),
            pltpu.VMEM((max(count for _, count in WAYS) * PER_CHUNK, BLOCK, BLOCK), f32),
            pltpu.VMEM((1, NA), i32),
            pltpu.VMEM((1, NC), i32),
            pltpu.SMEM((1, NA), i32),
            pltpu.SMEM((1, NC), i32),
            pltpu.VMEM((KSET, 2 * BLOCK, CB * BLOCK), bf16),
            pltpu.VMEM((NA * CB, BLOCK, BLOCK), f32),
            pltpu.VMEM((NC, BLOCK, BLOCK), f32),
            pltpu.VMEM((NC, BLOCK, BLOCK), f32),
            pltpu.VMEM((max(reps - 1, 1), share, BLOCK, BLOCK), f32),
            pltpu.VMEM((reps, share, BLOCK, BLOCK), f32),
            pltpu.VMEM((reps, 1, BLOCK, BLOCK), f32),
            pltpu.VMEM((1, BLOCK, BLOCK), f32),
            pltpu.SMEM((NB,), i32),
            pltpu.SMEM((NA,), i32),
            pltpu.SMEM((NB,), i32),
            pltpu.SMEM((NA,), i32),
            dma((2,)), dma((2,)), dma((2,)), dma((2,)), dma((CHUNKS,)), dma((CHUNKS,)),
            dma((max(count for _, count in WAYS),)), dma((max(count for _, count in WAYS),)),
            dma((max(reps - 1, 1),)), dma((max(reps - 1, 1),)), dma((reps,)), dma((reps,)), dma((reps,)), dma((reps,)), dma, dma,
        ],
        compiler_params=pltpu.CompilerParams(
            collective_id=0, has_side_effects=True, vmem_limit_bytes=60 * 1024 * 1024
        ),
        cost_estimate=pl.CostEstimate(flops=2 * 2 * NA * 4 * CB * BLOCK**3, bytes_accessed=4 << 20, transcendentals=0),
    )(
        a_spots, b_spots, c_spots,
        a_blocks.reshape(NA, BLOCK, BLOCK), b_blocks.reshape(NB, BLOCK, BLOCK), a_spots, c_spots,
    )
    return result[None, None]


def solution(mesh):
    in_specs = (
        P("row", "col", "rep", None, None, None),
        P("row", "col", "rep", None),
        P("row", "col", "rep", None, None, None),
        P("row", "col", "rep", None),
        P("row", "col", None),
    )
    out_specs = P("row", "col", "rep", None, None)
    body = functools.partial(shards, mesh.shape["row"], mesh.shape["col"], mesh.shape["rep"])
    return jax.shard_map(body, mesh=mesh, in_specs=in_specs, out_specs=out_specs, check_vma=False)
```
